32 devices in a mesh: dp: 8 (over z, x), fsdp: 4 (over y, core).
Axes of the slice: x: 2, y: 2, z: 4, core: 2. Of those that a mesh axis runs over, the one named last changes fastest.
Arguments:
- tokens: bfloat16 [1024, 4096], P('dp', 'fsdp'), may hold values from -6 to 6
- expert_ids: int32 [1024, 2], P('dp'), may hold values from 0 to 7, all different within a row; in each aligned block of 128 rows (0 to 127, 128 to 255, ...) at most 40 rows name the same one
- route_probs: float32 [1024, 2], P('dp'), may hold values from 0.1 to 0.9
- w_gate: bfloat16 [4096, 65536], P(None, ('dp', 'fsdp')), may hold values from -0.09375 to 0.09375
- w_up: bfloat16 [4096, 65536], P(None, ('dp', 'fsdp')), may hold values from -0.09375 to 0.09375
- w_down: bfloat16 [65536, 4096], P(('dp', 'fsdp')), may hold values from -0.0625 to 0.0625
- out_grad: bfloat16 [1024, 4096], P('dp', 'fsdp'), may hold values from -0.59765625 to 0.59765625
Outputs:
- mixed: bfloat16 [1024, 4096], P('dp', 'fsdp')
- token_grad: bfloat16 [1024, 4096], P('dp', 'fsdp')
- prob_grad: float32 [1024, 2], P('dp')
- gate_weight_grad: bfloat16 [4096, 65536], P(None, ('dp', 'fsdp'))
- up_weight_grad: bfloat16 [4096, 65536], P(None, ('dp', 'fsdp'))
- down_weight_grad: bfloat16 [65536, 4096], P(('dp', 'fsdp'))
The draws below stay inside these ranges and needn't reach their ends.
Inputs may be any that keep to these rules, and one draw needn't show every extreme that they name: `expert_ids`: each token names two different experts. Within the 128 tokens of one dp index (aligned blocks of rows) no expert is named more than 40 times, and in some block one expert is named exactly 40 times.
All inputs are finite; a program needn't handle non-finite values.
Results may differ from the reference program's by a relative error of at most 0.019.
Values may be sent and summed in bfloat16 or wider, within the bound.
A program may use at most 192 MiB of HBM per device.

```python
import math
import jax
import jax.numpy as jnp
import numpy as np
from jax import lax

D = 4096
E = 8
FF = 8192
TOK_DP = 128
CAP = 40
TOKENS = 1024
HID_DEV = 2048
N_DP = 8


def levels(key, extent, split, smallest, top_value):
    def one(dim, shards_of):
        draws = jax.random.uniform(jax.random.fold_in(jax.random.fold_in(key, 6), dim), (shards_of,), jnp.float32, smallest / len(split), top_value / len(split))
        return jnp.repeat(jnp.exp(draws), extent[dim] // shards_of).reshape((-1,) + (1,) * (len(extent) - dim - 1))

    level = one(*split[0])
    for cut in split[1:]:
        level = level * one(*cut)
    return level


def assign_block(key, own, number, rows, amount, top, limit, skew):
    sequence = jax.random.permutation(key, amount)
    heavy_load, common = portions_of(amount, rows * top, limit, skew, True), portions_of(amount, rows * top, limit, skew, False)
    places = jnp.arange(amount)

    def named(lengths, rotation):
        used = int((lengths > 0).sum())
        fixed = max(1, used // 4)
        moved = fixed + (places - fixed + rotation * (used - fixed)) % max(1, amount - fixed)
        return jnp.zeros((amount,), jnp.int32).at[sequence[jnp.where(places < fixed, places, moved)]].set(jnp.asarray(lengths, jnp.int32))

    lengths = jnp.where(number % 4 == 0, named(heavy_load, number // 4), named(common, number - number // 4 - 1))
    mixed = jax.random.permutation(jax.random.fold_in(own, 3), amount)
    donor, receiver = mixed[0:amount // 2 * 2:2], mixed[1:amount // 2 * 2:2]
    room = jnp.minimum(lengths[donor] - 1, limit - lengths[receiver]) // 2
    room = jnp.where((donor == sequence[0]) | (receiver == sequence[0]) | (lengths[receiver] == 0), 0, jnp.maximum(room, 0))
    moved = jax.random.randint(jax.random.fold_in(own, 4), (amount // 2,), 0, 1 << 20) % (room + 1)
    lengths = lengths.at[donor].add(-moved).at[receiver].add(moved)
    labels = jnp.searchsorted(jnp.cumsum(lengths), jnp.arange(rows * top), side="right").astype(jnp.int32)
    grid = labels.reshape(top, rows).T
    grid = grid[jax.random.permutation(jax.random.fold_in(own, 1), rows)]
    rotation = jax.random.randint(jax.random.fold_in(own, 2), (rows, 1), 0, top)
    return jnp.take_along_axis(grid, (jnp.arange(top)[None, :] + rotation) % top, axis=1)


def portions_of(count, total, bound, skew, full):
    loads = [(1 << 20) // math.isqrt(grade ** skew) + 1 for grade in range(1, count + 1)]
    largest = bound if full else min(bound, max(-(-total // count), total * loads[0] // sum(loads)))
    least = 1 if total - largest >= count - 1 else 0
    given, spare = [largest] + [least] * (count - 1), total - largest - least * (count - 1)
    while spare > 0:
        free = [i for i in range(1, count) if given[i] < largest] or [i for i in range(1, count) if given[i] < bound]
        pool, remaining = sum([loads[i] for i in free]), spare
        for i in free:
            extra = min(bound - given[i], max(1, remaining * loads[i] // pool), spare)
            given[i] = given[i] + extra
            spare = spare - extra
    return np.array(given)


def normal_values(key, extent, width, most, split=(), held_as=jnp.bfloat16):
    values = jax.random.normal(key, extent, jnp.float32) * width
    if len(split) > 0:
        values = levels(key, extent, split, -0.22, 0.18) * values
    return jnp.clip(values, min=-most, max=most).astype(held_as)


def setup_inputs(seed: int = 0) -> dict:
    seeds = jax.random.split(jax.random.key(seed), 8)
    tokens = normal_values(seeds[0], (TOKENS, D), 1.0, 6.0, ((0, 8), (1, 4)))
    expert_ids_keys = jax.random.split(jax.random.fold_in(seeds[1], 1), TOKENS // TOK_DP)
    expert_ids_turns = jax.random.permutation(jax.random.fold_in(seeds[1], 3), TOKENS // TOK_DP)
    expert_ids = jax.vmap(lambda own, number: assign_block(jax.random.fold_in(seeds[1], 2), own, number, TOK_DP, E, 2, CAP, 2))(expert_ids_keys, expert_ids_turns).reshape((TOKENS, 2))
    route_probs = jnp.clip(0.1 + 0.79999997 * jax.random.uniform(seeds[2], (TOKENS, 2), jnp.float32) ** levels(seeds[2], (TOKENS, 2), ((0, 8),), -0.2, 0.2), 0.1, 0.9)
    w_gate = normal_values(seeds[3], (D, E * FF), D ** -0.5, 0.09375, ((1, 32),))
    w_up = normal_values(seeds[4], (D, E * FF), D ** -0.5, 0.09375, ((1, 32),))
    w_down = normal_values(seeds[5], (E * FF, D), FF ** -0.5, 0.0625, ((0, 32),))
    out_grad = normal_values(seeds[6], (TOKENS, D), 0.1, 0.59765625, ((0, 8), (1, 4)))
    return dict(tokens=tokens, expert_ids=expert_ids, route_probs=route_probs, w_gate=w_gate, w_up=w_up, w_down=w_down, out_grad=out_grad)


def expert_pass(operands):
    expert_rows, grad_rows, gate_w, up_w, down_w = operands
    gate_proj = jnp.dot(expert_rows, gate_w, preferred_element_type=jnp.float32)
    up_proj = jnp.dot(expert_rows, up_w, preferred_element_type=jnp.float32)
    sigmoid_gate = jax.nn.sigmoid(gate_proj)
    activated = gate_proj * sigmoid_gate
    hidden = (activated * up_proj).astype(jnp.bfloat16)
    blocks = FF // HID_DEV
    row_count = expert_rows.shape[0]
    hidden_blocks = hidden.reshape(row_count, blocks, HID_DEV).transpose(1, 0, 2)
    down_blocks = down_w.reshape(blocks, HID_DEV, D)

    def add_output(total, pieces):
        piece_hidden, piece_down = pieces
        term = jnp.dot(piece_hidden, piece_down, preferred_element_type=jnp.float32).astype(jnp.bfloat16)
        term = lax.optimization_barrier(term)
        return total + term.astype(jnp.float32), None

    outputs, unused = lax.scan(add_output, jnp.zeros((row_count, D), jnp.float32), (hidden_blocks, down_blocks))
    hidden_grad = lax.dot_general(grad_rows, down_w, (((1,), (1,)), ((), ())), preferred_element_type=jnp.float32)
    gate_grad = (hidden_grad * up_proj * sigmoid_gate * (1.0 + gate_proj * (1.0 - sigmoid_gate))).astype(jnp.bfloat16)
    up_grad = (hidden_grad * activated).astype(jnp.bfloat16)
    contract_rows = (((0,), (0,)), ((), ()))
    gate_w_grad = lax.dot_general(expert_rows, gate_grad, contract_rows, preferred_element_type=jnp.float32).astype(jnp.bfloat16)
    up_w_grad = lax.dot_general(expert_rows, up_grad, contract_rows, preferred_element_type=jnp.float32).astype(jnp.bfloat16)
    down_w_grad = lax.dot_general(hidden, grad_rows, contract_rows, preferred_element_type=jnp.float32).astype(jnp.bfloat16)
    gate_blocks = gate_w.reshape(D, blocks, HID_DEV).transpose(1, 0, 2)
    up_blocks = up_w.reshape(D, blocks, HID_DEV).transpose(1, 0, 2)
    gate_grad_blocks = gate_grad.reshape(row_count, blocks, HID_DEV).transpose(1, 0, 2)
    up_grad_blocks = up_grad.reshape(row_count, blocks, HID_DEV).transpose(1, 0, 2)
    back_dims = (((1,), (1,)), ((), ()))

    def add_input(total, pieces):
        piece_gate, piece_up, weight_gate, weight_up = pieces
        term = lax.dot_general(piece_gate, weight_gate, back_dims, preferred_element_type=jnp.float32)
        term = term + lax.dot_general(piece_up, weight_up, back_dims, preferred_element_type=jnp.float32)
        term = lax.optimization_barrier(term.astype(jnp.bfloat16))
        return total + term.astype(jnp.float32), None

    inputs_grad, unused = lax.scan(add_input, jnp.zeros((row_count, D), jnp.float32),
                                   (gate_grad_blocks, up_grad_blocks, gate_blocks, up_blocks))
    return outputs, inputs_grad, gate_w_grad, up_w_grad, down_w_grad


def reference(tokens, expert_ids, route_probs, w_gate, w_up, w_down, out_grad):
    pair_count = TOKENS * 2
    routing = expert_ids.reshape(-1).astype(jnp.int32)
    onehot = (routing[:, None] == jnp.arange(E, dtype=jnp.int32)[None, :]).astype(jnp.int32)
    position = jnp.sum((jnp.cumsum(onehot, axis=0) - onehot) * onehot, axis=1).astype(jnp.int32)
    capacity = N_DP * CAP
    slot_of = (routing * capacity + position).astype(jnp.int32)
    token_of = (jnp.arange(pair_count, dtype=jnp.int32) // 2).astype(jnp.int32)
    token_table = jnp.zeros((E * capacity,), jnp.int32).at[slot_of].set(token_of)
    live_rows = jnp.zeros((E * capacity,), jnp.float32).at[slot_of].set(1.0)
    prob_table = jnp.zeros((E * capacity,), jnp.float32).at[slot_of].set(route_probs.reshape(-1))
    expert_rows = (tokens[token_table].astype(jnp.float32) * live_rows[:, None]).astype(jnp.bfloat16)
    grad_rows = (out_grad[token_table].astype(jnp.float32) * prob_table[:, None]).astype(jnp.bfloat16)
    gate_all = w_gate.reshape(D, E, FF).transpose(1, 0, 2)
    up_all = w_up.reshape(D, E, FF).transpose(1, 0, 2)
    down_all = w_down.reshape(E, FF, D)
    outputs, inputs_grad, gate_w_grad, up_w_grad, down_w_grad = lax.map(
        expert_pass,
        (expert_rows.reshape(E, capacity, D), grad_rows.reshape(E, capacity, D), gate_all, up_all, down_all))
    out_pairs = outputs.reshape(E * capacity, D)[slot_of].reshape(TOKENS, 2, D)
    mixed = jnp.sum(route_probs[:, :, None] * out_pairs, axis=1).astype(jnp.bfloat16)
    prob_grad = jnp.sum(out_pairs * out_grad.astype(jnp.float32)[:, None, :], axis=2)
    token_grad = jnp.sum(inputs_grad.reshape(E * capacity, D)[slot_of].reshape(TOKENS, 2, D), axis=1).astype(jnp.bfloat16)
    gate_weight_grad = gate_w_grad.transpose(1, 0, 2).reshape(D, E * FF)
    up_weight_grad = up_w_grad.transpose(1, 0, 2).reshape(D, E * FF)
    down_weight_grad = down_w_grad.reshape(E * FF, D)
    return (mixed, token_grad, prob_grad, gate_weight_grad, up_weight_grad, down_weight_grad)
```

```python
import jax
import jax.numpy as jnp
from jax import lax
from jax.sharding import PartitionSpec as P

E = 8
CAP = 40
BF = jnp.bfloat16
F32 = jnp.float32


def swap(value, bit):
    n = lax.axis_size("fsdp")
    return lax.ppermute(value, "fsdp", [(i, i ^ bit) for i in range(n)])


def gather_features(shard):
    n = lax.axis_size("fsdp")
    if n & (n - 1):
        return lax.all_gather(shard, "fsdp", axis=1, tiled=True)
    width = shard.shape[1]
    me = lax.axis_index("fsdp")
    held, offsets = [shard], [0]
    bit = n // 2
    while bit:
        held = held + [swap(h, bit) for h in held]
        offsets = offsets + [o ^ bit for o in offsets]
        bit //= 2
    full = jnp.zeros((shard.shape[0], width * n), shard.dtype)
    for piece, offset in zip(held, offsets):
        full = lax.dynamic_update_slice(full, piece, (0, (me ^ offset) * width))
    return full


def scatter_features(partial):
    n = lax.axis_size("fsdp")
    if n & (n - 1):
        return lax.psum_scatter(partial, "fsdp", scatter_dimension=1, tiled=True)
    width = partial.shape[1] // n
    me = lax.axis_index("fsdp")
    pieces = {
        o: lax.dynamic_slice(partial, (0, (me ^ o) * width), (partial.shape[0], width))
        for o in range(n)
    }
    bit = 1
    while bit < n:
        pieces = {
            o: (pieces[o].astype(F32) + swap(pieces[o ^ bit], bit).astype(F32)).astype(BF)
            for o in pieces
            if not o & bit
        }
        bit *= 2
    return pieces[0]


def local(tokens, expert_ids, route_probs, w_gate, w_up, w_down, out_grad):
    dp_count = lax.axis_size("dp")
    groups = dp_count // E
    token_count = tokens.shape[0]
    slot_total = E * CAP
    routing = expert_ids.reshape(-1)
    pair = jnp.arange(routing.shape[0], dtype=jnp.int32)
    earlier = jnp.logical_and(
        routing[:, None] == routing[None, :], pair[None, :] < pair[:, None]
    )
    position = jnp.sum(earlier.astype(jnp.int32), axis=1)
    slot_of = (routing * CAP + position).reshape(token_count, 2)
    slot_index = jnp.arange(slot_total, dtype=jnp.int32)
    select_first = slot_of[:, 0:1] == slot_index[None, :]
    select_second = slot_of[:, 1:2] == slot_index[None, :]
    picker = jnp.logical_or(select_first, select_second).astype(BF)
    slot_prob = jnp.sum(
        jnp.where(select_first, route_probs[:, 0:1], 0.0)
        + jnp.where(select_second, route_probs[:, 1:2], 0.0),
        axis=0,
    )
    contract_rows = (((0,), (0,)), ((), ()))
    back_dims = (((1,), (1,)), ((), ()))

    def to_expert_shard(source, scale):
        placed = lax.dot_general(picker, source, contract_rows, preferred_element_type=F32)
        if scale is not None:
            placed = placed * scale[:, None]
        placed = placed.astype(BF).reshape(E, CAP, source.shape[1])
        placed = jnp.repeat(placed, groups, axis=0)
        arrived = lax.all_to_all(placed, "dp", split_axis=0, concat_axis=0, tiled=True)
        return arrived.reshape(dp_count * CAP, arrived.shape[2])

    def to_token_layout(partial_value):
        shares = scatter_features(partial_value)
        returned = lax.all_to_all(
            shares.reshape(dp_count, CAP, shares.shape[1]),
            "dp",
            split_axis=0,
            concat_axis=0,
            tiled=True,
        )
        return returned.reshape(E, groups, CAP, returned.shape[2])

    def pick(select, slots):
        total = 0.0
        for g in range(groups):
            total = total + jnp.dot(
                select.astype(BF),
                slots[:, g].reshape(slot_total, slots.shape[3]),
                preferred_element_type=F32,
            )
        return total

    token_shard = to_expert_shard(tokens, None)
    grad_shard = to_expert_shard(out_grad, slot_prob)
    expert_rows = gather_features(token_shard)
    grad_rows = gather_features(grad_shard)
    gate_proj = jnp.dot(expert_rows, w_gate, preferred_element_type=F32)
    up_proj = jnp.dot(expert_rows, w_up, preferred_element_type=F32)
    sigmoid_gate = jax.nn.sigmoid(gate_proj)
    activated = gate_proj * sigmoid_gate
    hidden = (activated * up_proj).astype(BF)
    out_partial = jnp.dot(hidden, w_down, preferred_element_type=F32).astype(BF)
    out_slots = to_token_layout(out_partial)
    hidden_grad = lax.dot_general(grad_rows, w_down, back_dims, preferred_element_type=F32)
    gate_grad = (
        hidden_grad * up_proj * sigmoid_gate * (1.0 + gate_proj * (1.0 - sigmoid_gate))
    ).astype(BF)
    up_grad = (hidden_grad * activated).astype(BF)
    input_partial = lax.dot_general(gate_grad, w_gate, back_dims, preferred_element_type=F32)
    input_partial = input_partial + lax.dot_general(
        up_grad, w_up, back_dims, preferred_element_type=F32
    )
    input_slots = to_token_layout(input_partial.astype(BF))
    gate_weight_grad = lax.dot_general(
        expert_rows, gate_grad, contract_rows, preferred_element_type=F32
    ).astype(BF)
    up_weight_grad = lax.dot_general(
        expert_rows, up_grad, contract_rows, preferred_element_type=F32
    ).astype(BF)
    down_weight_grad = lax.dot_general(
        hidden, grad_rows, contract_rows, preferred_element_type=F32
    ).astype(BF)
    first_pair = pick(select_first, out_slots)
    second_pair = pick(select_second, out_slots)
    mixed = (route_probs[:, 0:1] * first_pair + route_probs[:, 1:2] * second_pair).astype(BF)
    grad_local = out_grad.astype(F32)
    prob_terms = jnp.stack(
        [jnp.sum(first_pair * grad_local, axis=1), jnp.sum(second_pair * grad_local, axis=1)],
        axis=1,
    )
    prob_grad = lax.psum(prob_terms, "fsdp")
    token_grad = pick(picker, input_slots).astype(BF)
    return (mixed, token_grad, prob_grad, gate_weight_grad, up_weight_grad, down_weight_grad)


def solution(mesh):
    placed = (
        P("dp", "fsdp"),
        P("dp", None),
        P("dp", None),
        P(None, ("dp", "fsdp")),
        P(None, ("dp", "fsdp")),
        P(("dp", "fsdp"), None),
        P("dp", "fsdp"),
    )
    return jax.shard_map(
        local,
        mesh=mesh,
        in_specs=placed,
        out_specs=(
            P("dp", "fsdp"),
            P("dp", "fsdp"),
            P("dp", None),
            P(None, ("dp", "fsdp")),
            P(None, ("dp", "fsdp")),
            P(("dp", "fsdp"), None),
        ),
        check_vma=False,
    )
```

```python
import jax
import jax.numpy as jnp
from jax import lax
from jax.experimental import pallas as pl
from jax.experimental.pallas import tpu as pltpu
from jax.sharding import PartitionSpec as P

E = 8
CAP = 40
BF = jnp.bfloat16
F32 = jnp.float32


CONTRACT_ROWS = (((0,), (0,)), ((), ()))
BACK_DIMS = (((1,), (1,)), ((), ()))
VMEM = 40 << 20


def input_body(gate_grad, up_grad, w_gate, w_up, out):
    total = lax.dot_general(gate_grad[...], w_gate[...], BACK_DIMS, preferred_element_type=F32)
    total += lax.dot_general(up_grad[...], w_up[...], BACK_DIMS, preferred_element_type=F32)
    out[...] = total.astype(BF)


def input_sum(gate_grad, up_grad, w_gate, w_up):
    rows, hid = gate_grad.shape
    features = w_gate.shape[0]
    step = min(1024, features)
    whole = pl.BlockSpec((rows, hid), lambda i: (0, 0))
    block = pl.BlockSpec((step, hid), lambda i: (i, 0))
    return pl.pallas_call(
        input_body,
        grid=(features // step,),
        in_specs=[whole, whole, block, block],
        out_specs=pl.BlockSpec((rows, step), lambda i: (0, i)),
        out_shape=jax.ShapeDtypeStruct((rows, features), BF),
        compiler_params=pltpu.CompilerParams(vmem_limit_bytes=VMEM),
        cost_estimate=pl.CostEstimate(
            flops=4 * rows * hid * features,
            bytes_accessed=4 * features * hid + 4 * rows * hid + 2 * rows * features,
            transcendentals=0,
        ),
    )(gate_grad, up_grad, w_gate, w_up)


def weight_body(left, *refs):
    half = len(refs) // 2
    for right, out in zip(refs[:half], refs[half:]):
        out[...] = lax.dot_general(
            left[...], right[...], CONTRACT_ROWS, preferred_element_type=F32
        ).astype(BF)


def weight_grads(left, rights, step):
    rows, columns = left.shape
    width = rights[0].shape[1]
    n = len(rights)
    step = min(step, columns)
    return pl.pallas_call(
        weight_body,
        grid=(columns // step,),
        in_specs=[pl.BlockSpec((rows, step), lambda i: (0, i))]
        + [pl.BlockSpec((rows, width), lambda i: (0, 0))] * n,
        out_specs=[pl.BlockSpec((step, width), lambda i: (i, 0))] * n,
        out_shape=[jax.ShapeDtypeStruct((columns, width), BF)] * n,
        compiler_params=pltpu.CompilerParams(vmem_limit_bytes=VMEM),
        cost_estimate=pl.CostEstimate(
            flops=2 * n * rows * columns * width,
            bytes_accessed=2 * n * columns * width + 2 * rows * (columns + n * width),
            transcendentals=0,
        ),
    )(left, *rights)


def swap(value, bit):
    n = lax.axis_size("fsdp")
    return lax.ppermute(value, "fsdp", [(i, i ^ bit) for i in range(n)])


def gather_features(shard, after=None):
    n = lax.axis_size("fsdp")
    if n & (n - 1):
        return lax.all_gather(shard, "fsdp", axis=1, tiled=True), after
    width = shard.shape[1]
    me = lax.axis_index("fsdp")
    held, offsets = [shard], [0]
    bit = n // 2
    while bit:
        held = held + [swap(h, bit) for h in held]
        offsets = offsets + [o ^ bit for o in offsets]
        if after is not None and bit == n // 2:
            held, after = lax.optimization_barrier((held, after))
        bit //= 2
    full = jnp.zeros((shard.shape[0], width * n), shard.dtype)
    for piece, offset in zip(held, offsets):
        full = lax.dynamic_update_slice(full, piece, (0, (me ^ offset) * width))
    return full, after


def scatter_features(partial, after=None):
    n = lax.axis_size("fsdp")
    if n & (n - 1):
        return lax.psum_scatter(partial, "fsdp", scatter_dimension=1, tiled=True), after
    width = partial.shape[1] // n
    me = lax.axis_index("fsdp")
    pieces = {
        o: lax.dynamic_slice(partial, (0, (me ^ o) * width), (partial.shape[0], width))
        for o in range(n)
    }
    bit = 1
    while bit < n:
        pieces = {
            o: (pieces[o].astype(F32) + swap(pieces[o ^ bit], bit).astype(F32)).astype(BF)
            for o in pieces
            if not o & bit
        }
        if after is not None and bit == 1:
            pieces, after = lax.optimization_barrier((pieces, after))
        bit *= 2
    return pieces[0], after


def sum_features(value):
    n = lax.axis_size("fsdp")
    if n & (n - 1):
        return lax.psum(value, "fsdp")
    bit = 1
    while bit < n:
        value = value + swap(value, bit)
        bit *= 2
    return value


def local(tokens, expert_ids, route_probs, w_gate, w_up, w_down, out_grad):
    dp_count = lax.axis_size("dp")
    groups = dp_count // E
    token_count = tokens.shape[0]
    slot_total = E * CAP
    routing = expert_ids.reshape(-1)
    pair = jnp.arange(routing.shape[0], dtype=jnp.int32)
    earlier = jnp.logical_and(
        routing[:, None] == routing[None, :], pair[None, :] < pair[:, None]
    )
    position = jnp.sum(earlier.astype(jnp.int32), axis=1)
    slot_of = (routing * CAP + position).reshape(token_count, 2)
    slot_index = jnp.arange(slot_total, dtype=jnp.int32)
    select_first = slot_of[:, 0:1] == slot_index[None, :]
    select_second = slot_of[:, 1:2] == slot_index[None, :]
    picker = jnp.logical_or(select_first, select_second).astype(BF)
    slot_prob = jnp.sum(
        jnp.where(select_first, route_probs[:, 0:1], 0.0)
        + jnp.where(select_second, route_probs[:, 1:2], 0.0),
        axis=0,
    )

    def to_expert_shard(source, scale):
        placed = lax.dot_general(picker, source, CONTRACT_ROWS, preferred_element_type=F32)
        if scale is not None:
            placed = placed * scale[:, None]
        placed = placed.astype(BF).reshape(E, CAP, source.shape[1])
        placed = jnp.repeat(placed, groups, axis=0)
        arrived = lax.all_to_all(placed, "dp", split_axis=0, concat_axis=0, tiled=True)
        return arrived.reshape(dp_count * CAP, arrived.shape[2])

    def to_token_layout(shares):
        returned = lax.all_to_all(
            shares.reshape(dp_count, CAP, shares.shape[1]),
            "dp",
            split_axis=0,
            concat_axis=0,
            tiled=True,
        )
        return returned.reshape(E, groups, CAP, returned.shape[2])

    def pick(select, slots):
        total = 0.0
        for g in range(groups):
            total = total + jnp.dot(
                select.astype(BF),
                slots[:, g].reshape(slot_total, slots.shape[3]),
                preferred_element_type=F32,
            )
        return total

    token_shard = to_expert_shard(tokens, None)
    grad_shard = to_expert_shard(out_grad, slot_prob)
    expert_rows, _ = gather_features(token_shard)
    gate_proj = jnp.dot(expert_rows, w_gate, preferred_element_type=F32)
    gate_proj, grad_shard = lax.optimization_barrier((gate_proj, grad_shard))
    up_proj = jnp.dot(expert_rows, w_up, preferred_element_type=F32)
    sigmoid_gate = jax.nn.sigmoid(gate_proj)
    activated = gate_proj * sigmoid_gate
    hidden = (activated * up_proj).astype(BF)
    grad_rows, hidden = gather_features(grad_shard, hidden)
    out_partial = jnp.dot(hidden, w_down, preferred_element_type=F32).astype(BF)
    hidden_grad = lax.dot_general(grad_rows, w_down, BACK_DIMS, preferred_element_type=F32)
    gate_grad = (
        hidden_grad * up_proj * sigmoid_gate * (1.0 + gate_proj * (1.0 - sigmoid_gate))
    ).astype(BF)
    up_grad = (hidden_grad * activated).astype(BF)
    out_shares, gate_grad = scatter_features(out_partial, gate_grad)
    input_partial = input_sum(gate_grad, up_grad, w_gate, w_up)
    out_slots = to_token_layout(out_shares)
    input_slots = to_token_layout(scatter_features(input_partial)[0])
    gate_weight_grad, up_weight_grad = weight_grads(expert_rows, [gate_grad, up_grad], 512)
    down_weight_grad = lax.dot_general(
        hidden, grad_rows, CONTRACT_ROWS, preferred_element_type=F32
    ).astype(BF)
    first_pair = pick(select_first, out_slots)
    second_pair = pick(select_second, out_slots)
    mixed = (route_probs[:, 0:1] * first_pair + route_probs[:, 1:2] * second_pair).astype(BF)
    grad_local = out_grad.astype(F32)
    prob_terms = jnp.stack(
        [jnp.sum(first_pair * grad_local, axis=1), jnp.sum(second_pair * grad_local, axis=1)],
        axis=1,
    )
    prob_grad = sum_features(prob_terms)
    token_grad = pick(picker, input_slots).astype(BF)
    return (mixed, token_grad, prob_grad, gate_weight_grad, up_weight_grad, down_weight_grad)


def solution(mesh):
    placed = (
        P("dp", "fsdp"),
        P("dp", None),
        P("dp", None),
        P(None, ("dp", "fsdp")),
        P(None, ("dp", "fsdp")),
        P(("dp", "fsdp"), None),
        P("dp", "fsdp"),
    )
    return jax.shard_map(
        local,
        mesh=mesh,
        in_specs=placed,
        out_specs=(
            P("dp", "fsdp"),
            P("dp", "fsdp"),
            P("dp", None),
            P(None, ("dp", "fsdp")),
            P(None, ("dp", "fsdp")),
            P(("dp", "fsdp"), None),
        ),
        check_vma=False,
    )
```
